32 devices in a mesh: sens: 8 (over z, y), unk: 4 (over x, core).
Axes of the slice: x: 2, y: 2, z: 4, core: 2. Of those that a mesh axis runs over, the one named last changes fastest.
Arguments:
- signals: float32 [256, 4, 256], P('sens', None, 'unk'), may hold values from -6 to 6
- kernel: float32 [256, 32, 4096], P('sens', None, 'unk'), may hold values from -0.046875 to 0.046875
- tap_weights: float32 [17, 4096], P(None, 'unk'), may hold values from -1.5 to 1.5
Outputs:
- hessian_action: float32 [256, 4, 256], P('sens', None, 'unk')
The draws below stay inside these ranges and needn't reach their ends.
All inputs are finite; a program needn't handle non-finite values.
Results may differ from the reference program's by a relative error of at most 0.00008.
Values sent between devices are 32-bit elements; how exact they have to be, the bound alone decides.
A program may use at most 64 MiB of HBM per device.

```python
import jax
import jax.numpy as jnp
from jax import lax

LAGS = 32
T_SIZE = 256
NVEC = 4
HALF = 8
TAPS = 17
SENSORS = 256
UNKNOWNS = 4096


def shard_levels(own_key, shape, cuts, least, largest):
    gain = 1.0
    for position, blocks in cuts:
        heights = jax.random.uniform(jax.random.fold_in(jax.random.fold_in(own_key, 6), position), (blocks,), jnp.float32, least / len(cuts), largest / len(cuts))
        gain = gain * jnp.repeat(jnp.exp(heights), shape[position] // blocks).reshape((-1,) + (1,) * (len(shape) - 1 - position))
    return gain


def gaussian(own_key, shape, deviation, limit, split=(), dtype=jnp.bfloat16):
    array = deviation * jax.random.normal(own_key, shape, jnp.float32)
    if split:
        array = array * shard_levels(own_key, shape, split, -0.22, 0.18)
    return jnp.clip(array, -limit, limit).astype(dtype)


def setup_inputs(seed: int = 0) -> dict:
    streams_of = jax.random.split(jax.random.key(seed), 4)
    signals = gaussian(streams_of[0], (SENSORS, NVEC, T_SIZE), 1.0, 6.0, ((0, 8), (2, 4)), jnp.float32)
    kernel = gaussian(streams_of[1], (SENSORS, LAGS, UNKNOWNS), (LAGS * (SENSORS + UNKNOWNS) // 8) ** -0.5, 0.046875, ((0, 8), (2, 4)), jnp.float32)
    tap_weights = gaussian(streams_of[2], (TAPS, UNKNOWNS), TAPS ** -0.5, 1.5, ((1, 4),), jnp.float32)
    return dict(signals=signals, kernel=kernel, tap_weights=tap_weights)


def hankel(signals, lag_count):
    steps_count = signals.shape[2]
    padded = jnp.pad(signals, ((0, 0), (0, 0), (0, lag_count)))
    return jnp.stack([padded[:, :, offset:offset + steps_count] for offset in range(lag_count)], axis=1)


def skew_sum(product):
    sens_rows, vectors, lag_count, steps_count = product.shape
    padded = jnp.pad(product, ((0, 0), (0, 0), (0, 0), (0, lag_count)))
    flattened = padded.reshape(sens_rows, vectors, lag_count * (steps_count + lag_count))
    flattened = flattened[:, :, :lag_count * (steps_count + lag_count - 1)]
    sheared = flattened.reshape(sens_rows, vectors, lag_count, steps_count + lag_count - 1)
    return jnp.sum(sheared[..., :steps_count], axis=2)


def smooth_time(series, tap_weights, half_width):
    steps_count = series.shape[2]
    padded = jnp.pad(series, ((0, 0), (0, 0), (half_width, half_width)))
    result = jnp.zeros(series.shape, jnp.float32)
    for tap_index in range(2 * half_width + 1):
        result = result + tap_weights[tap_index][:, None, None] * padded[:, :, tap_index:tap_index + steps_count]
    return result


def reference(signals, kernel, tap_weights):
    window = hankel(signals, LAGS)
    adjoint = jnp.einsum('slu,slbt->ubt', kernel, window, precision=lax.Precision.HIGHEST)
    smoothed = smooth_time(adjoint, tap_weights, HALF)
    product = jnp.einsum('slu,ubt->sblt', kernel, smoothed, precision=lax.Precision.HIGHEST)
    return skew_sum(product)
```

```python
import functools

import jax
import jax.numpy as jnp
from jax import lax
from jax.experimental import pallas as pl
from jax.experimental.pallas import tpu as pltpu
from jax.sharding import PartitionSpec as P

MESH = pl.DeviceIdType.MESH
VMEM_LIMIT = 56 * 1024 * 1024
HOP = 2


def hankel(signals, lag_count):
    steps_count = signals.shape[2]
    padded = jnp.pad(signals, ((0, 0), (0, 0), (0, lag_count)))
    return jnp.stack(
        [padded[:, :, offset : offset + steps_count] for offset in range(lag_count)], axis=1
    )


def greet(axis, peers):
    barrier = pltpu.get_barrier_semaphore()
    for peer in peers:
        pl.semaphore_signal(barrier, inc=1, device_id={axis: peer}, device_id_type=MESH)
    pl.semaphore_wait(barrier, len(peers))


def split(x):
    high = x.astype(jnp.bfloat16)
    return high, (x - high.astype(jnp.float32)).astype(jnp.bfloat16)


def smooth_rows(x, taps, steps_count):
    tap_count = taps.shape[1]
    half = (tap_count - 1) // 2
    pieces = []
    for first in range(0, x.shape[1], steps_count):
        part = x[:, first : first + steps_count]
        time = lax.broadcasted_iota(jnp.int32, part.shape, 1)
        total = taps[:, half : half + 1] * part
        for tap in range(tap_count):
            offset = tap - half
            if offset == 0:
                continue
            moved = pltpu.roll(part, (-offset) % steps_count, 1)
            inside = (time < steps_count - offset) if offset > 0 else (time >= -offset)
            total = total + taps[:, tap : tap + 1] * jnp.where(inside, moved, 0.0)
        pieces.append(total)
    return jnp.concatenate(pieces, axis=1)


def sum_kernel(chain, chunks, steps_count, p_ref, tap_ref, out_ref, y_in, own, up_in, up_out,
               down_in, down_out, sems):
    n = 2 * chain
    me = lax.axis_index("sens")
    z, y = me // 2, me % 2
    mate = z * 2 + (1 - y)
    above, below = jnp.minimum(me + 2, n - 1), jnp.maximum(me - 2, 0)
    half_rows = p_ref.shape[0] // 2
    rows = half_rows // chunks
    not_last, not_first = z < chain - 1, z > 0

    def chunk(c):
        return pl.ds(pl.multiple_of(c * rows, rows), rows)

    def half_chunk(h, c):
        return pl.ds(pl.multiple_of(h * half_rows + c * rows, rows), rows)

    def y_copy(c):
        return pltpu.make_async_remote_copy(
            src_ref=p_ref.at[half_chunk(1 - y, c)], dst_ref=y_in.at[chunk(c)],
            send_sem=sems.at[0, c], recv_sem=sems.at[1, c],
            device_id={"sens": mate}, device_id_type=MESH)

    def up_copy(c):
        return pltpu.make_async_remote_copy(
            src_ref=up_out.at[chunk(c)], dst_ref=up_in.at[chunk(c)],
            send_sem=sems.at[2, c], recv_sem=sems.at[3, c],
            device_id={"sens": above}, device_id_type=MESH)

    def down_copy(c):
        return pltpu.make_async_remote_copy(
            src_ref=down_out.at[chunk(c)], dst_ref=down_in.at[chunk(c)],
            send_sem=sems.at[4, c], recv_sem=sems.at[5, c],
            device_id={"sens": below}, device_id_type=MESH)

    def back_copy(c):
        part = out_ref.at[half_chunk(y, c)]
        return pltpu.make_async_remote_copy(
            src_ref=part, dst_ref=part,
            send_sem=sems.at[6, c], recv_sem=sems.at[7, c],
            device_id={"sens": mate}, device_id_type=MESH)

    def back_wait(c):
        part = out_ref.at[half_chunk(1 - y, c)]
        pltpu.make_async_remote_copy(
            src_ref=part, dst_ref=part,
            send_sem=sems.at[6, c], recv_sem=sems.at[7, c],
            device_id={"sens": mate}, device_id_type=MESH).wait_recv()

    barrier = pltpu.get_barrier_semaphore()
    pl.semaphore_signal(barrier, inc=1, device_id={"sens": mate}, device_id_type=MESH)

    @pl.when(not_last)
    def _():
        pl.semaphore_signal(barrier, inc=1, device_id={"sens": above}, device_id_type=MESH)

    @pl.when(not_first)
    def _():
        pl.semaphore_signal(barrier, inc=1, device_id={"sens": below}, device_id_type=MESH)

    pl.semaphore_wait(barrier, 1 + jnp.where(not_last, 1, 0) + jnp.where(not_first, 1, 0))

    @pl.loop(0, chunks)
    def _(c):
        y_copy(c).start()

    lag_up, lag_down = HOP * z, HOP * (chain - 1 - z)
    lag_last = HOP * (chain - 1)

    @pl.loop(0, chunks + lag_last)
    def _(step):
        @pl.when(step < chunks)
        def _():
            y_copy(step).wait_recv()
            own[chunk(step)] = p_ref[half_chunk(y, step)] + y_in[chunk(step)]

        up = step - lag_up

        @pl.when((up >= 0) & (up < chunks))
        def _():
            @pl.when(not_first)
            def _():
                up_copy(up).wait_recv()

            @pl.when(jnp.logical_not(not_first))
            def _():
                up_in[chunk(up)] = jnp.zeros((rows, p_ref.shape[1]), jnp.float32)

            @pl.when(not_last)
            def _():
                up_out[chunk(up)] = own[chunk(up)] + up_in[chunk(up)]
                up_copy(up).start()

        down = step - lag_down

        @pl.when((down >= 0) & (down < chunks))
        def _():
            @pl.when(not_last)
            def _():
                down_copy(down).wait_recv()

            @pl.when(jnp.logical_not(not_last))
            def _():
                down_in[chunk(down)] = jnp.zeros((rows, p_ref.shape[1]), jnp.float32)

            @pl.when(not_first)
            def _():
                down_out[chunk(down)] = own[chunk(down)] + down_in[chunk(down)]
                down_copy(down).start()

        last = step - lag_last

        @pl.when((last >= 0) & (last < chunks))
        def _():
            total = own[chunk(last)] + up_in[chunk(last)] + down_in[chunk(last)]
            out_ref[half_chunk(y, last)] = smooth_rows(
                total, tap_ref[half_chunk(y, last)], steps_count
            )
            back_copy(last).start()

    @pl.loop(0, chunks)
    def _(c):
        y_copy(c).wait_send()
        back_copy(c).wait_send()
        back_wait(c)

        @pl.when(not_last)
        def _():
            up_copy(c).wait_send()

        @pl.when(not_first)
        def _():
            down_copy(c).wait_send()


def summed_smoothed(partial, taps, steps_count, sens_count):
    unk_dev, columns = partial.shape
    chunks = max(1, unk_dev // 2 // 32)
    half = pltpu.VMEM((unk_dev // 2, columns), jnp.float32)
    return pl.pallas_call(
        functools.partial(sum_kernel, sens_count // 2, chunks, steps_count),
        out_shape=jax.ShapeDtypeStruct(partial.shape, jnp.float32),
        in_specs=[pl.BlockSpec(memory_space=pltpu.VMEM)] * 2,
        out_specs=pl.BlockSpec(memory_space=pltpu.VMEM),
        scratch_shapes=[half] * 6 + [pltpu.SemaphoreType.DMA((8, chunks))],
        compiler_params=pltpu.CompilerParams(
            collective_id=0, has_side_effects=True, vmem_limit_bytes=VMEM_LIMIT
        ),
    )(partial, taps)


def forward_kernel(lag_count, vectors, k_ref, s_ref, out_ref, high, low):
    @pl.when(pl.program_id(0) == 0)
    def _():
        high[...], low[...] = split(s_ref[...])

    k_high, k_low = split(k_ref[...])
    dot = functools.partial(jnp.dot, preferred_element_type=jnp.float32)
    steps_count = s_ref.shape[1] // vectors
    time = lax.broadcasted_iota(jnp.int32, (lag_count, steps_count), 1)
    lag = lax.broadcasted_iota(jnp.int32, (lag_count, steps_count), 0)
    for vector in range(vectors):
        columns = slice(vector * steps_count, (vector + 1) * steps_count)
        product = dot(k_high, high[:, columns]) + (
            dot(k_high, low[:, columns]) + dot(k_low, high[:, columns])
        )
        for sensor in range(k_ref.shape[0] // lag_count):
            part = product[sensor * lag_count : (sensor + 1) * lag_count]
            sheared = pltpu.roll(part, 0, 1, stride=1, stride_axis=0)
            row = jnp.sum(jnp.where(time >= lag, sheared, 0.0), axis=0, keepdims=True)
            place = sensor * vectors + vector
            out_ref[place : place + 1, :] = row


def forward(kernel, smoothed, lag_count, vectors):
    rows, unk_dev = kernel.shape
    columns = smoothed.shape[1]
    group = min(8, rows // lag_count)
    sens_rows = rows // lag_count
    return pl.pallas_call(
        functools.partial(forward_kernel, lag_count, vectors),
        grid=(sens_rows // group,),
        out_shape=jax.ShapeDtypeStruct((sens_rows * vectors, columns // vectors), jnp.float32),
        in_specs=[
            pl.BlockSpec((group * lag_count, unk_dev), lambda i: (i, 0)),
            pl.BlockSpec((unk_dev, columns), lambda i: (0, 0)),
        ],
        out_specs=pl.BlockSpec((group * vectors, columns // vectors), lambda i: (i, 0)),
        scratch_shapes=[pltpu.VMEM((unk_dev, columns), jnp.bfloat16)] * 2,
        compiler_params=pltpu.CompilerParams(vmem_limit_bytes=VMEM_LIMIT),
    )(kernel, smoothed)


def scatter_kernel(n, x_ref, out_ref, stage, landed, send_sem, recv_sem):
    me = lax.axis_index("unk")
    width = out_ref.shape[1]
    greet("unk", [lax.rem(me + k, n) for k in range(1, n)])
    for piece in range(n):
        stage[piece] = x_ref[:, piece * width : (piece + 1) * width]

    def copy(k):
        peer = lax.rem(me + k, n)
        return pltpu.make_async_remote_copy(
            src_ref=stage.at[peer], dst_ref=landed.at[k],
            send_sem=send_sem.at[k], recv_sem=recv_sem.at[k],
            device_id={"unk": peer}, device_id_type=MESH)

    for k in range(1, n):
        copy(k).start()
    total = stage[me]
    for k in range(1, n):
        copy(k).wait_recv()
        total = total + landed[k]
    out_ref[...] = total
    for k in range(1, n):
        copy(k).wait_send()


def scattered(partial, n):
    rows, steps_count = partial.shape
    width = steps_count // n
    return pl.pallas_call(
        functools.partial(scatter_kernel, n),
        out_shape=jax.ShapeDtypeStruct((rows, width), jnp.float32),
        in_specs=[pl.BlockSpec(memory_space=pltpu.VMEM)],
        out_specs=pl.BlockSpec(memory_space=pltpu.VMEM),
        scratch_shapes=[
            pltpu.VMEM((n, rows, width), jnp.float32),
            pltpu.VMEM((n, rows, width), jnp.float32),
            pltpu.SemaphoreType.DMA((n,)),
            pltpu.SemaphoreType.DMA((n,)),
        ],
        compiler_params=pltpu.CompilerParams(
            collective_id=1, has_side_effects=True, vmem_limit_bytes=VMEM_LIMIT
        ),
    )(partial)


def on_device(signals, kernel, tap_weights, *, sens_count, unk_count):
    whole_signals = lax.all_gather(signals, "unk", axis=2, tiled=True)
    sens_rows, lag_count, unk_dev = kernel.shape
    _, vectors, steps_count = whole_signals.shape
    flat_kernel = kernel.reshape(sens_rows * lag_count, unk_dev)
    window = hankel(whole_signals, lag_count)
    window = window.reshape(sens_rows * lag_count, vectors * steps_count)
    partial = jnp.einsum("ku,kt->ut", flat_kernel, window, precision=lax.Precision.HIGH)
    smoothed = summed_smoothed(partial, tap_weights.T, steps_count, sens_count)
    product = forward(flat_kernel, smoothed, lag_count, vectors)
    return scattered(product, unk_count).reshape(signals.shape)


def solution(mesh):
    return jax.shard_map(
        functools.partial(
            on_device, sens_count=mesh.shape["sens"], unk_count=mesh.shape["unk"]
        ),
        mesh=mesh,
        in_specs=(P("sens", None, "unk"), P("sens", None, "unk"), P(None, "unk")),
        out_specs=P("sens", None, "unk"),
        check_vma=False,
    )
```

```python
import functools

import jax
import jax.numpy as jnp
from jax import lax
from jax.experimental import pallas as pl
from jax.experimental.pallas import tpu as pltpu
from jax.sharding import PartitionSpec as P

MESH = pl.DeviceIdType.MESH
VMEM_LIMIT = 56 * 1024 * 1024
HOP = 2


def greet(axis, peers):
    barrier = pltpu.get_barrier_semaphore()
    for peer in peers:
        pl.semaphore_signal(barrier, inc=1, device_id={axis: peer}, device_id_type=MESH)
    pl.semaphore_wait(barrier, len(peers))


def split(x):
    high = x.astype(jnp.bfloat16)
    return high, (x - high.astype(jnp.float32)).astype(jnp.bfloat16)


def smooth_rows(x, taps, steps_count):
    tap_count = taps.shape[1]
    half = (tap_count - 1) // 2
    pieces = []
    for first in range(0, x.shape[1], steps_count):
        part = x[:, first : first + steps_count]
        time = lax.broadcasted_iota(jnp.int32, part.shape, 1)
        total = taps[:, half : half + 1] * part
        for tap in range(tap_count):
            offset = tap - half
            if offset == 0:
                continue
            moved = pltpu.roll(part, (-offset) % steps_count, 1)
            inside = (time < steps_count - offset) if offset > 0 else (time >= -offset)
            total = total + taps[:, tap : tap + 1] * jnp.where(inside, moved, 0.0)
        pieces.append(total)
    return jnp.concatenate(pieces, axis=1)


def sum_kernel(chain, chunks, steps_count, p_ref, tap_ref, out_ref, y_in, own, up_in, up_out,
               down_in, down_out, sems):
    n = 2 * chain
    me = lax.axis_index("sens")
    z, y = me // 2, me % 2
    mate = z * 2 + (1 - y)
    above, below = jnp.minimum(me + 2, n - 1), jnp.maximum(me - 2, 0)
    half_rows = p_ref.shape[0] // 2
    rows = half_rows // chunks
    not_last, not_first = z < chain - 1, z > 0

    def chunk(c):
        return pl.ds(pl.multiple_of(c * rows, rows), rows)

    def half_chunk(h, c):
        return pl.ds(pl.multiple_of(h * half_rows + c * rows, rows), rows)

    def y_copy(c):
        return pltpu.make_async_remote_copy(
            src_ref=p_ref.at[half_chunk(1 - y, c)], dst_ref=y_in.at[chunk(c)],
            send_sem=sems.at[0, c], recv_sem=sems.at[1, c],
            device_id={"sens": mate}, device_id_type=MESH)

    def up_copy(c):
        return pltpu.make_async_remote_copy(
            src_ref=up_out.at[chunk(c)], dst_ref=up_in.at[chunk(c)],
            send_sem=sems.at[2, c], recv_sem=sems.at[3, c],
            device_id={"sens": above}, device_id_type=MESH)

    def down_copy(c):
        return pltpu.make_async_remote_copy(
            src_ref=down_out.at[chunk(c)], dst_ref=down_in.at[chunk(c)],
            send_sem=sems.at[4, c], recv_sem=sems.at[5, c],
            device_id={"sens": below}, device_id_type=MESH)

    def back_copy(c):
        part = out_ref.at[half_chunk(y, c)]
        return pltpu.make_async_remote_copy(
            src_ref=part, dst_ref=part,
            send_sem=sems.at[6, c], recv_sem=sems.at[7, c],
            device_id={"sens": mate}, device_id_type=MESH)

    def back_wait(c):
        part = out_ref.at[half_chunk(1 - y, c)]
        pltpu.make_async_remote_copy(
            src_ref=part, dst_ref=part,
            send_sem=sems.at[6, c], recv_sem=sems.at[7, c],
            device_id={"sens": mate}, device_id_type=MESH).wait_recv()

    barrier = pltpu.get_barrier_semaphore()
    pl.semaphore_signal(barrier, inc=1, device_id={"sens": mate}, device_id_type=MESH)

    @pl.when(not_last)
    def _():
        pl.semaphore_signal(barrier, inc=1, device_id={"sens": above}, device_id_type=MESH)

    @pl.when(not_first)
    def _():
        pl.semaphore_signal(barrier, inc=1, device_id={"sens": below}, device_id_type=MESH)

    pl.semaphore_wait(barrier, 1 + jnp.where(not_last, 1, 0) + jnp.where(not_first, 1, 0))

    @pl.loop(0, chunks)
    def _(c):
        y_copy(c).start()

    lag_up, lag_down = HOP * z, HOP * (chain - 1 - z)
    lag_last = HOP * (chain - 1)

    @pl.loop(0, chunks + lag_last)
    def _(step):
        @pl.when(step < chunks)
        def _():
            y_copy(step).wait_recv()
            own[chunk(step)] = p_ref[half_chunk(y, step)] + y_in[chunk(step)]

        up = step - lag_up

        @pl.when((up >= 0) & (up < chunks))
        def _():
            @pl.when(not_first)
            def _():
                up_copy(up).wait_recv()

            @pl.when(jnp.logical_not(not_first))
            def _():
                up_in[chunk(up)] = jnp.zeros((rows, p_ref.shape[1]), jnp.float32)

            @pl.when(not_last)
            def _():
                up_out[chunk(up)] = own[chunk(up)] + up_in[chunk(up)]
                up_copy(up).start()

        down = step - lag_down

        @pl.when((down >= 0) & (down < chunks))
        def _():
            @pl.when(not_last)
            def _():
                down_copy(down).wait_recv()

            @pl.when(jnp.logical_not(not_last))
            def _():
                down_in[chunk(down)] = jnp.zeros((rows, p_ref.shape[1]), jnp.float32)

            @pl.when(not_first)
            def _():
                down_out[chunk(down)] = own[chunk(down)] + down_in[chunk(down)]
                down_copy(down).start()

        last = step - lag_last

        @pl.when((last >= 0) & (last < chunks))
        def _():
            total = own[chunk(last)] + up_in[chunk(last)] + down_in[chunk(last)]
            out_ref[half_chunk(y, last)] = smooth_rows(
                total, tap_ref[half_chunk(y, last)], steps_count
            )
            back_copy(last).start()

    @pl.loop(0, chunks)
    def _(c):
        y_copy(c).wait_send()
        back_copy(c).wait_send()
        back_wait(c)

        @pl.when(not_last)
        def _():
            up_copy(c).wait_send()

        @pl.when(not_first)
        def _():
            down_copy(c).wait_send()


def summed_smoothed(partial, taps, steps_count, sens_count):
    unk_dev, columns = partial.shape
    chunks = max(1, unk_dev // 2 // 32)
    half = pltpu.VMEM((unk_dev // 2, columns), jnp.float32)
    return pl.pallas_call(
        functools.partial(sum_kernel, sens_count // 2, chunks, steps_count),
        out_shape=jax.ShapeDtypeStruct(partial.shape, jnp.float32),
        in_specs=[pl.BlockSpec(memory_space=pltpu.VMEM)] * 2,
        out_specs=pl.BlockSpec(memory_space=pltpu.VMEM),
        scratch_shapes=[half] * 6 + [pltpu.SemaphoreType.DMA((8, chunks))],
        compiler_params=pltpu.CompilerParams(
            collective_id=0, has_side_effects=True, vmem_limit_bytes=VMEM_LIMIT
        ),
    )(partial, taps)


def gather_kernel(n, x_ref, out_ref, landed, send_sem, recv_sem):
    me = lax.axis_index("unk")
    width = x_ref.shape[1]
    greet("unk", [lax.rem(me + k, n) for k in range(1, n)])

    def copy(k):
        peer = lax.rem(me + k, n)
        return pltpu.make_async_remote_copy(
            src_ref=x_ref, dst_ref=landed.at[me],
            send_sem=send_sem.at[k], recv_sem=recv_sem.at[k],
            device_id={"unk": peer}, device_id_type=MESH)

    for k in range(1, n):
        copy(k).start()
    landed[me] = x_ref[...]
    for k in range(1, n):
        copy(k).wait_recv()
    for piece in range(n):
        out_ref[:, piece * width : (piece + 1) * width] = landed[piece]
    for k in range(1, n):
        copy(k).wait_send()


def gathered(part, n):
    rows, width = part.shape
    return pl.pallas_call(
        functools.partial(gather_kernel, n),
        out_shape=jax.ShapeDtypeStruct((rows, n * width), jnp.float32),
        in_specs=[pl.BlockSpec(memory_space=pltpu.VMEM)],
        out_specs=pl.BlockSpec(memory_space=pltpu.VMEM),
        scratch_shapes=[
            pltpu.VMEM((n, rows, width), jnp.float32),
            pltpu.SemaphoreType.DMA((n,)),
            pltpu.SemaphoreType.DMA((n,)),
        ],
        compiler_params=pltpu.CompilerParams(
            collective_id=2, has_side_effects=True, vmem_limit_bytes=VMEM_LIMIT
        ),
    )(part)


def adjoint_kernel(lag_count, vectors, sig_ref, k_ref, out_ref, high, low):
    steps_count = sig_ref.shape[1]

    @pl.when(pl.program_id(0) == 0)
    def _():
        time = lax.broadcasted_iota(jnp.int32, (lag_count, steps_count), 1)
        lag = lax.broadcasted_iota(jnp.int32, (lag_count, steps_count), 0)

        @pl.loop(0, sig_ref.shape[0] // vectors)
        def _(sensor):
            rows = pl.ds(pl.multiple_of(sensor * lag_count, lag_count), lag_count)
            for vector in range(vectors):
                series = sig_ref[pl.ds(sensor * vectors + vector, 1), :]
                moved = jnp.broadcast_to(series, (lag_count, steps_count))
                bit = 1
                while bit < lag_count:
                    moved = jnp.where(
                        (lag & bit) != 0, pltpu.roll(moved, steps_count - bit, 1), moved
                    )
                    bit *= 2
                columns = slice(vector * steps_count, (vector + 1) * steps_count)
                moved = jnp.where(time + lag < steps_count, moved, 0.0)
                high[rows, columns], low[rows, columns] = split(moved)

    k_high, k_low = split(k_ref[...].T)
    dot = functools.partial(jnp.dot, preferred_element_type=jnp.float32)
    for vector in range(vectors):
        columns = slice(vector * steps_count, (vector + 1) * steps_count)
        out_ref[:, columns] = dot(k_high, high[:, columns]) + (
            dot(k_high, low[:, columns]) + dot(k_low, high[:, columns])
        )


def adjoint(series, kernel, lag_count, vectors):
    rows, unk_dev = kernel.shape
    steps_count = series.shape[1]
    tile = min(256, unk_dev)
    return pl.pallas_call(
        functools.partial(adjoint_kernel, lag_count, vectors),
        grid=(unk_dev // tile,),
        out_shape=jax.ShapeDtypeStruct((unk_dev, vectors * steps_count), jnp.float32),
        in_specs=[
            pl.BlockSpec(series.shape, lambda i: (0, 0)),
            pl.BlockSpec((rows, tile), lambda i: (0, i)),
        ],
        out_specs=pl.BlockSpec((tile, vectors * steps_count), lambda i: (i, 0)),
        scratch_shapes=[pltpu.VMEM((rows, vectors * steps_count), jnp.bfloat16)] * 2,
        compiler_params=pltpu.CompilerParams(vmem_limit_bytes=VMEM_LIMIT),
    )(series, kernel)


def forward_kernel(lag_count, vectors, k_ref, s_ref, out_ref, high, low):
    @pl.when(pl.program_id(0) == 0)
    def _():
        high[...], low[...] = split(s_ref[...])

    k_high, k_low = split(k_ref[...])
    dot = functools.partial(jnp.dot, preferred_element_type=jnp.float32)
    steps_count = s_ref.shape[1] // vectors
    time = lax.broadcasted_iota(jnp.int32, (lag_count, steps_count), 1)
    lag = lax.broadcasted_iota(jnp.int32, (lag_count, steps_count), 0)
    for vector in range(vectors):
        columns = slice(vector * steps_count, (vector + 1) * steps_count)
        product = dot(k_high, high[:, columns]) + (
            dot(k_high, low[:, columns]) + dot(k_low, high[:, columns])
        )
        for sensor in range(k_ref.shape[0] // lag_count):
            part = product[sensor * lag_count : (sensor + 1) * lag_count]
            sheared = pltpu.roll(part, 0, 1, stride=1, stride_axis=0)
            row = jnp.sum(jnp.where(time >= lag, sheared, 0.0), axis=0, keepdims=True)
            place = sensor * vectors + vector
            out_ref[place : place + 1, :] = row


def forward(kernel, smoothed, lag_count, vectors):
    rows, unk_dev = kernel.shape
    columns = smoothed.shape[1]
    group = min(8, rows // lag_count)
    sens_rows = rows // lag_count
    return pl.pallas_call(
        functools.partial(forward_kernel, lag_count, vectors),
        grid=(sens_rows // group,),
        out_shape=jax.ShapeDtypeStruct((sens_rows * vectors, columns // vectors), jnp.float32),
        in_specs=[
            pl.BlockSpec((group * lag_count, unk_dev), lambda i: (i, 0)),
            pl.BlockSpec((unk_dev, columns), lambda i: (0, 0)),
        ],
        out_specs=pl.BlockSpec((group * vectors, columns // vectors), lambda i: (i, 0)),
        scratch_shapes=[pltpu.VMEM((unk_dev, columns), jnp.bfloat16)] * 2,
        compiler_params=pltpu.CompilerParams(vmem_limit_bytes=VMEM_LIMIT),
    )(kernel, smoothed)


def scatter_kernel(n, x_ref, out_ref, stage, landed, send_sem, recv_sem):
    me = lax.axis_index("unk")
    width = out_ref.shape[1]
    greet("unk", [lax.rem(me + k, n) for k in range(1, n)])
    for piece in range(n):
        stage[piece] = x_ref[:, piece * width : (piece + 1) * width]

    def copy(k):
        peer = lax.rem(me + k, n)
        return pltpu.make_async_remote_copy(
            src_ref=stage.at[peer], dst_ref=landed.at[k],
            send_sem=send_sem.at[k], recv_sem=recv_sem.at[k],
            device_id={"unk": peer}, device_id_type=MESH)

    for k in range(1, n):
        copy(k).start()
    total = stage[me]
    for k in range(1, n):
        copy(k).wait_recv()
        total = total + landed[k]
    out_ref[...] = total
    for k in range(1, n):
        copy(k).wait_send()


def scattered(partial, n):
    rows, steps_count = partial.shape
    width = steps_count // n
    return pl.pallas_call(
        functools.partial(scatter_kernel, n),
        out_shape=jax.ShapeDtypeStruct((rows, width), jnp.float32),
        in_specs=[pl.BlockSpec(memory_space=pltpu.VMEM)],
        out_specs=pl.BlockSpec(memory_space=pltpu.VMEM),
        scratch_shapes=[
            pltpu.VMEM((n, rows, width), jnp.float32),
            pltpu.VMEM((n, rows, width), jnp.float32),
            pltpu.SemaphoreType.DMA((n,)),
            pltpu.SemaphoreType.DMA((n,)),
        ],
        compiler_params=pltpu.CompilerParams(
            collective_id=1, has_side_effects=True, vmem_limit_bytes=VMEM_LIMIT
        ),
    )(partial)


def on_device(signals, kernel, tap_weights, *, sens_count, unk_count):
    sens_rows, lag_count, unk_dev = kernel.shape
    _, vectors, width = signals.shape
    steps_count = width * unk_count
    series = gathered(signals.reshape(sens_rows * vectors, width), unk_count)
    flat_kernel = kernel.reshape(sens_rows * lag_count, unk_dev)
    partial = adjoint(series, flat_kernel, lag_count, vectors)
    smoothed = summed_smoothed(partial, tap_weights.T, steps_count, sens_count)
    product = forward(flat_kernel, smoothed, lag_count, vectors)
    return scattered(product, unk_count).reshape(signals.shape)


def solution(mesh):
    return jax.shard_map(
        functools.partial(
            on_device, sens_count=mesh.shape["sens"], unk_count=mesh.shape["unk"]
        ),
        mesh=mesh,
        in_specs=(P("sens", None, "unk"), P("sens", None, "unk"), P(None, "unk")),
        out_specs=P("sens", None, "unk"),
        check_vma=False,
    )
```

```python
import functools

import jax
import jax.numpy as jnp
from jax import lax
from jax.experimental import pallas as pl
from jax.experimental.pallas import tpu as pltpu
from jax.sharding import PartitionSpec as P

MESH = pl.DeviceIdType.MESH
VMEM_LIMIT = 56 * 1024 * 1024
HOP = 2


def greet(axis, peers):
    barrier = pltpu.get_barrier_semaphore()
    for peer in peers:
        pl.semaphore_signal(barrier, inc=1, device_id={axis: peer}, device_id_type=MESH)
    pl.semaphore_wait(barrier, len(peers))


def split(x):
    high = x.astype(jnp.bfloat16)
    return high, (x - high.astype(jnp.float32)).astype(jnp.bfloat16)


def smooth_rows(x, taps, steps_count):
    tap_count = taps.shape[1]
    half = (tap_count - 1) // 2
    pieces = []
    for first in range(0, x.shape[1], steps_count):
        part = x[:, first : first + steps_count]
        time = lax.broadcasted_iota(jnp.int32, part.shape, 1)
        total = taps[:, half : half + 1] * part
        for tap in range(tap_count):
            offset = tap - half
            if offset == 0:
                continue
            moved = pltpu.roll(part, (-offset) % steps_count, 1)
            inside = (time < steps_count - offset) if offset > 0 else (time >= -offset)
            total = total + taps[:, tap : tap + 1] * jnp.where(inside, moved, 0.0)
        pieces.append(total)
    return jnp.concatenate(pieces, axis=1)


def build_window(lag_count, vectors, sig_ref, high, low):
    steps_count = sig_ref.shape[1]
    time = lax.broadcasted_iota(jnp.int32, (lag_count, steps_count), 1)
    lag = lax.broadcasted_iota(jnp.int32, (lag_count, steps_count), 0)

    @pl.loop(0, sig_ref.shape[0] // vectors)
    def _(sensor):
        rows = pl.ds(pl.multiple_of(sensor * lag_count, lag_count), lag_count)
        for vector in range(vectors):
            series = sig_ref[pl.ds(sensor * vectors + vector, 1), :]
            moved = jnp.broadcast_to(series, (lag_count, steps_count))
            bit = 1
            while bit < lag_count:
                moved = jnp.where(
                    (lag & bit) != 0, pltpu.roll(moved, steps_count - bit, 1), moved
                )
                bit *= 2
            columns = slice(vector * steps_count, (vector + 1) * steps_count)
            moved = jnp.where(time + lag < steps_count, moved, 0.0)
            high[rows, columns], low[rows, columns] = split(moved)


def adjoint_tile(kernel_tile, steps_count, high, low, p_ref, rows):
    k_high, k_low = split(kernel_tile.T)
    dot = functools.partial(jnp.dot, preferred_element_type=jnp.float32)
    for first in range(0, high.shape[1], steps_count):
        columns = slice(first, first + steps_count)
        p_ref[rows, columns] = dot(k_high, high[:, columns]) + (
            dot(k_high, low[:, columns]) + dot(k_low, high[:, columns])
        )


def sum_kernel(chain, chunks, lag_count, vectors, tile, sig_ref, k_ref, tap_ref, out_ref, y_in,
               own, up_in, up_out, down_in, down_out, p_ref, high, low, sems):
    steps_count = sig_ref.shape[1]
    n = 2 * chain
    me = lax.axis_index("sens")
    z, y = me // 2, me % 2
    mate = z * 2 + (1 - y)
    above, below = jnp.minimum(me + 2, n - 1), jnp.maximum(me - 2, 0)
    half_rows = p_ref.shape[0] // 2
    rows = half_rows // chunks
    not_last, not_first = z < chain - 1, z > 0

    def chunk(c):
        return pl.ds(pl.multiple_of(c * rows, rows), rows)

    def half_chunk(h, c):
        return pl.ds(pl.multiple_of(h * half_rows + c * rows, rows), rows)

    def y_copy(c):
        return pltpu.make_async_remote_copy(
            src_ref=p_ref.at[half_chunk(1 - y, c)], dst_ref=y_in.at[chunk(c)],
            send_sem=sems.at[0, c], recv_sem=sems.at[1, c],
            device_id={"sens": mate}, device_id_type=MESH)

    def up_copy(c):
        return pltpu.make_async_remote_copy(
            src_ref=up_out.at[chunk(c)], dst_ref=up_in.at[chunk(c)],
            send_sem=sems.at[2, c], recv_sem=sems.at[3, c],
            device_id={"sens": above}, device_id_type=MESH)

    def down_copy(c):
        return pltpu.make_async_remote_copy(
            src_ref=down_out.at[chunk(c)], dst_ref=down_in.at[chunk(c)],
            send_sem=sems.at[4, c], recv_sem=sems.at[5, c],
            device_id={"sens": below}, device_id_type=MESH)

    def back_copy(c):
        part = out_ref.at[half_chunk(y, c)]
        return pltpu.make_async_remote_copy(
            src_ref=part, dst_ref=part,
            send_sem=sems.at[6, c], recv_sem=sems.at[7, c],
            device_id={"sens": mate}, device_id_type=MESH)

    def back_wait(c):
        part = out_ref.at[half_chunk(1 - y, c)]
        pltpu.make_async_remote_copy(
            src_ref=part, dst_ref=part,
            send_sem=sems.at[6, c], recv_sem=sems.at[7, c],
            device_id={"sens": mate}, device_id_type=MESH).wait_recv()

    barrier = pltpu.get_barrier_semaphore()
    pl.semaphore_signal(barrier, inc=1, device_id={"sens": mate}, device_id_type=MESH)

    @pl.when(not_last)
    def _():
        pl.semaphore_signal(barrier, inc=1, device_id={"sens": above}, device_id_type=MESH)

    @pl.when(not_first)
    def _():
        pl.semaphore_signal(barrier, inc=1, device_id={"sens": below}, device_id_type=MESH)

    pl.semaphore_wait(barrier, 1 + jnp.where(not_last, 1, 0) + jnp.where(not_first, 1, 0))

    build_window(lag_count, vectors, sig_ref, high, low)

    @pl.loop(0, half_rows // tile)
    def _(part):
        place = pl.ds(pl.multiple_of((1 - y) * half_rows + part * tile, tile), tile)
        adjoint_tile(k_ref[:, place], steps_count, high, low, p_ref, place)

        @pl.loop(0, tile // rows)
        def _(c):
            y_copy(part * (tile // rows) + c).start()

    @pl.loop(0, half_rows // tile)
    def _(part):
        place = pl.ds(pl.multiple_of(y * half_rows + part * tile, tile), tile)
        adjoint_tile(k_ref[:, place], steps_count, high, low, p_ref, place)

    lag_up, lag_down = HOP * z, HOP * (chain - 1 - z)
    lag_last = HOP * (chain - 1)

    @pl.loop(0, chunks + lag_last)
    def _(step):
        @pl.when(step < chunks)
        def _():
            y_copy(step).wait_recv()
            own[chunk(step)] = p_ref[half_chunk(y, step)] + y_in[chunk(step)]

        up = step - lag_up

        @pl.when((up >= 0) & (up < chunks))
        def _():
            @pl.when(not_first)
            def _():
                up_copy(up).wait_recv()

            @pl.when(jnp.logical_not(not_first))
            def _():
                up_in[chunk(up)] = jnp.zeros((rows, p_ref.shape[1]), jnp.float32)

            @pl.when(not_last)
            def _():
                up_out[chunk(up)] = own[chunk(up)] + up_in[chunk(up)]
                up_copy(up).start()

        down = step - lag_down

        @pl.when((down >= 0) & (down < chunks))
        def _():
            @pl.when(not_last)
            def _():
                down_copy(down).wait_recv()

            @pl.when(jnp.logical_not(not_last))
            def _():
                down_in[chunk(down)] = jnp.zeros((rows, p_ref.shape[1]), jnp.float32)

            @pl.when(not_first)
            def _():
                down_out[chunk(down)] = own[chunk(down)] + down_in[chunk(down)]
                down_copy(down).start()

        last = step - lag_last

        @pl.when((last >= 0) & (last < chunks))
        def _():
            total = own[chunk(last)] + up_in[chunk(last)] + down_in[chunk(last)]
            out_ref[half_chunk(y, last)] = smooth_rows(
                total, tap_ref[half_chunk(y, last)], steps_count
            )
            back_copy(last).start()

    @pl.loop(0, chunks)
    def _(c):
        y_copy(c).wait_send()
        back_copy(c).wait_send()
        back_wait(c)

        @pl.when(not_last)
        def _():
            up_copy(c).wait_send()

        @pl.when(not_first)
        def _():
            down_copy(c).wait_send()


def summed_smoothed(series, kernel, taps, lag_count, vectors, sens_count):
    rows, unk_dev = kernel.shape
    columns = vectors * series.shape[1]
    tile = 128
    chunks = max(1, unk_dev // 2 // 32)
    half = pltpu.VMEM((unk_dev // 2, columns), jnp.float32)
    return pl.pallas_call(
        functools.partial(sum_kernel, sens_count // 2, chunks, lag_count, vectors, tile),
        out_shape=jax.ShapeDtypeStruct((unk_dev, columns), jnp.float32),
        in_specs=[pl.BlockSpec(memory_space=pltpu.VMEM)] * 3,
        out_specs=pl.BlockSpec(memory_space=pltpu.VMEM),
        scratch_shapes=[half] * 6
        + [pltpu.VMEM((unk_dev, columns), jnp.float32)]
        + [pltpu.VMEM((rows, columns), jnp.bfloat16)] * 2
        + [pltpu.SemaphoreType.DMA((8, chunks))],
        compiler_params=pltpu.CompilerParams(
            collective_id=0, has_side_effects=True, vmem_limit_bytes=VMEM_LIMIT
        ),
    )(series, kernel, taps)


def gather_kernel(n, x_ref, out_ref, landed, send_sem, recv_sem):
    me = lax.axis_index("unk")
    width = x_ref.shape[1]
    greet("unk", [lax.rem(me + k, n) for k in range(1, n)])

    def copy(k):
        peer = lax.rem(me + k, n)
        return pltpu.make_async_remote_copy(
            src_ref=x_ref, dst_ref=landed.at[me],
            send_sem=send_sem.at[k], recv_sem=recv_sem.at[k],
            device_id={"unk": peer}, device_id_type=MESH)

    for k in range(1, n):
        copy(k).start()
    landed[me] = x_ref[...]
    for k in range(1, n):
        copy(k).wait_recv()
    for piece in range(n):
        out_ref[:, piece * width : (piece + 1) * width] = landed[piece]
    for k in range(1, n):
        copy(k).wait_send()


def gathered(part, n):
    rows, width = part.shape
    return pl.pallas_call(
        functools.partial(gather_kernel, n),
        out_shape=jax.ShapeDtypeStruct((rows, n * width), jnp.float32),
        in_specs=[pl.BlockSpec(memory_space=pltpu.VMEM)],
        out_specs=pl.BlockSpec(memory_space=pltpu.VMEM),
        scratch_shapes=[
            pltpu.VMEM((n, rows, width), jnp.float32),
            pltpu.SemaphoreType.DMA((n,)),
            pltpu.SemaphoreType.DMA((n,)),
        ],
        compiler_params=pltpu.CompilerParams(
            collective_id=2, has_side_effects=True, vmem_limit_bytes=VMEM_LIMIT
        ),
    )(part)


def forward_kernel(lag_count, vectors, k_ref, s_ref, out_ref, high, low):
    @pl.when(pl.program_id(0) == 0)
    def _():
        high[...], low[...] = split(s_ref[...])

    k_high, k_low = split(k_ref[...])
    dot = functools.partial(jnp.dot, preferred_element_type=jnp.float32)
    steps_count = s_ref.shape[1] // vectors
    time = lax.broadcasted_iota(jnp.int32, (lag_count, steps_count), 1)
    lag = lax.broadcasted_iota(jnp.int32, (lag_count, steps_count), 0)
    for vector in range(vectors):
        columns = slice(vector * steps_count, (vector + 1) * steps_count)
        product = dot(k_high, high[:, columns]) + (
            dot(k_high, low[:, columns]) + dot(k_low, high[:, columns])
        )
        for sensor in range(k_ref.shape[0] // lag_count):
            part = product[sensor * lag_count : (sensor + 1) * lag_count]
            sheared = pltpu.roll(part, 0, 1, stride=1, stride_axis=0)
            row = jnp.sum(jnp.where(time >= lag, sheared, 0.0), axis=0, keepdims=True)
            place = sensor * vectors + vector
            out_ref[place : place + 1, :] = row


def forward(kernel, smoothed, lag_count, vectors):
    rows, unk_dev = kernel.shape
    columns = smoothed.shape[1]
    group = min(8, rows // lag_count)
    sens_rows = rows // lag_count
    return pl.pallas_call(
        functools.partial(forward_kernel, lag_count, vectors),
        grid=(sens_rows // group,),
        out_shape=jax.ShapeDtypeStruct((sens_rows * vectors, columns // vectors), jnp.float32),
        in_specs=[
            pl.BlockSpec((group * lag_count, unk_dev), lambda i: (i, 0)),
            pl.BlockSpec((unk_dev, columns), lambda i: (0, 0)),
        ],
        out_specs=pl.BlockSpec((group * vectors, columns // vectors), lambda i: (i, 0)),
        scratch_shapes=[pltpu.VMEM((unk_dev, columns), jnp.bfloat16)] * 2,
        compiler_params=pltpu.CompilerParams(vmem_limit_bytes=VMEM_LIMIT),
    )(kernel, smoothed)


def scatter_kernel(n, x_ref, out_ref, stage, landed, send_sem, recv_sem):
    me = lax.axis_index("unk")
    width = out_ref.shape[1]
    greet("unk", [lax.rem(me + k, n) for k in range(1, n)])
    for piece in range(n):
        stage[piece] = x_ref[:, piece * width : (piece + 1) * width]

    def copy(k):
        peer = lax.rem(me + k, n)
        return pltpu.make_async_remote_copy(
            src_ref=stage.at[peer], dst_ref=landed.at[k],
            send_sem=send_sem.at[k], recv_sem=recv_sem.at[k],
            device_id={"unk": peer}, device_id_type=MESH)

    for k in range(1, n):
        copy(k).start()
    total = stage[me]
    for k in range(1, n):
        copy(k).wait_recv()
        total = total + landed[k]
    out_ref[...] = total
    for k in range(1, n):
        copy(k).wait_send()


def scattered(partial, n):
    rows, steps_count = partial.shape
    width = steps_count // n
    return pl.pallas_call(
        functools.partial(scatter_kernel, n),
        out_shape=jax.ShapeDtypeStruct((rows, width), jnp.float32),
        in_specs=[pl.BlockSpec(memory_space=pltpu.VMEM)],
        out_specs=pl.BlockSpec(memory_space=pltpu.VMEM),
        scratch_shapes=[
            pltpu.VMEM((n, rows, width), jnp.float32),
            pltpu.VMEM((n, rows, width), jnp.float32),
            pltpu.SemaphoreType.DMA((n,)),
            pltpu.SemaphoreType.DMA((n,)),
        ],
        compiler_params=pltpu.CompilerParams(
            collective_id=1, has_side_effects=True, vmem_limit_bytes=VMEM_LIMIT
        ),
    )(partial)


def on_device(signals, kernel, tap_weights, *, sens_count, unk_count):
    sens_rows, lag_count, unk_dev = kernel.shape
    _, vectors, width = signals.shape
    series = gathered(signals.reshape(sens_rows * vectors, width), unk_count)
    flat_kernel = kernel.reshape(sens_rows * lag_count, unk_dev)
    smoothed = summed_smoothed(
        series, flat_kernel, tap_weights.T, lag_count, vectors, sens_count
    )
    product = forward(flat_kernel, smoothed, lag_count, vectors)
    return scattered(product, unk_count).reshape(signals.shape)


def solution(mesh):
    return jax.shard_map(
        functools.partial(
            on_device, sens_count=mesh.shape["sens"], unk_count=mesh.shape["unk"]
        ),
        mesh=mesh,
        in_specs=(P("sens", None, "unk"), P("sens", None, "unk"), P(None, "unk")),
        out_specs=P("sens", None, "unk"),
        check_vma=False,
    )
```

```python
import functools

import jax
import jax.numpy as jnp
from jax import lax
from jax.experimental import pallas as pl
from jax.experimental.pallas import tpu as pltpu
from jax.sharding import PartitionSpec as P

MESH = pl.DeviceIdType.MESH
VMEM_LIMIT = 56 * 1024 * 1024
HOP = 2


def greet(axis, peers):
    barrier = pltpu.get_barrier_semaphore()
    for peer in peers:
        pl.semaphore_signal(barrier, inc=1, device_id={axis: peer}, device_id_type=MESH)
    pl.semaphore_wait(barrier, len(peers))


def split(x):
    high = x.astype(jnp.bfloat16)
    return high, (x - high.astype(jnp.float32)).astype(jnp.bfloat16)


def smooth_rows(x, taps, steps_count):
    tap_count = taps.shape[1]
    half = (tap_count - 1) // 2
    pieces = []
    for first in range(0, x.shape[1], steps_count):
        part = x[:, first : first + steps_count]
        time = lax.broadcasted_iota(jnp.int32, part.shape, 1)
        total = taps[:, half : half + 1] * part
        for tap in range(tap_count):
            offset = tap - half
            if offset == 0:
                continue
            moved = pltpu.roll(part, (-offset) % steps_count, 1)
            inside = (time < steps_count - offset) if offset > 0 else (time >= -offset)
            total = total + taps[:, tap : tap + 1] * jnp.where(inside, moved, 0.0)
        pieces.append(total)
    return jnp.concatenate(pieces, axis=1)


def build_window(lag_count, vectors, sig_ref, high, low):
    steps_count = sig_ref.shape[1]
    time = lax.broadcasted_iota(jnp.int32, (lag_count, steps_count), 1)
    lag = lax.broadcasted_iota(jnp.int32, (lag_count, steps_count), 0)

    @pl.loop(0, sig_ref.shape[0] // vectors)
    def _(sensor):
        rows = pl.ds(pl.multiple_of(sensor * lag_count, lag_count), lag_count)
        for vector in range(vectors):
            series = sig_ref[pl.ds(sensor * vectors + vector, 1), :]
            moved = jnp.broadcast_to(series, (lag_count, steps_count))
            bit = 1
            while bit < lag_count:
                moved = jnp.where(
                    (lag & bit) != 0, pltpu.roll(moved, steps_count - bit, 1), moved
                )
                bit *= 2
            columns = slice(vector * steps_count, (vector + 1) * steps_count)
            moved = jnp.where(time + lag < steps_count, moved, 0.0)
            high[rows, columns], low[rows, columns] = split(moved)


def adjoint_tile(kernel_tile, steps_count, high, low, p_ref, rows):
    k_high, k_low = split(kernel_tile.T)
    dot = functools.partial(jnp.dot, preferred_element_type=jnp.float32)
    for first in range(0, high.shape[1], steps_count):
        columns = slice(first, first + steps_count)
        p_ref[rows, columns] = dot(k_high, high[:, columns]) + (
            dot(k_high, low[:, columns]) + dot(k_low, high[:, columns])
        )


def sum_kernel(chain, chunks, lag_count, vectors, tile, sig_ref, k_ref, tap_ref, data_ref, y_in,
               own, up_in, up_out, down_in, down_out, p_ref, out_ref, high, low, s_high, s_low,
               product, sems):
    steps_count = sig_ref.shape[1]
    n = 2 * chain
    me = lax.axis_index("sens")
    z, y = me // 2, me % 2
    mate = z * 2 + (1 - y)
    above, below = jnp.minimum(me + 2, n - 1), jnp.maximum(me - 2, 0)
    half_rows = p_ref.shape[0] // 2
    rows = half_rows // chunks
    not_last, not_first = z < chain - 1, z > 0

    def chunk(c):
        return pl.ds(pl.multiple_of(c * rows, rows), rows)

    def half_chunk(h, c):
        return pl.ds(pl.multiple_of(h * half_rows + c * rows, rows), rows)

    def y_copy(c):
        return pltpu.make_async_remote_copy(
            src_ref=p_ref.at[half_chunk(1 - y, c)], dst_ref=y_in.at[chunk(c)],
            send_sem=sems.at[0, c], recv_sem=sems.at[1, c],
            device_id={"sens": mate}, device_id_type=MESH)

    def up_copy(c):
        return pltpu.make_async_remote_copy(
            src_ref=up_out.at[chunk(c)], dst_ref=up_in.at[chunk(c)],
            send_sem=sems.at[2, c], recv_sem=sems.at[3, c],
            device_id={"sens": above}, device_id_type=MESH)

    def down_copy(c):
        return pltpu.make_async_remote_copy(
            src_ref=down_out.at[chunk(c)], dst_ref=down_in.at[chunk(c)],
            send_sem=sems.at[4, c], recv_sem=sems.at[5, c],
            device_id={"sens": below}, device_id_type=MESH)

    def back_copy(c):
        part = out_ref.at[half_chunk(y, c)]
        return pltpu.make_async_remote_copy(
            src_ref=part, dst_ref=part,
            send_sem=sems.at[6, c], recv_sem=sems.at[7, c],
            device_id={"sens": mate}, device_id_type=MESH)

    def back_wait(c):
        part = out_ref.at[half_chunk(1 - y, c)]
        pltpu.make_async_remote_copy(
            src_ref=part, dst_ref=part,
            send_sem=sems.at[6, c], recv_sem=sems.at[7, c],
            device_id={"sens": mate}, device_id_type=MESH).wait_recv()

    barrier = pltpu.get_barrier_semaphore()
    pl.semaphore_signal(barrier, inc=1, device_id={"sens": mate}, device_id_type=MESH)

    @pl.when(not_last)
    def _():
        pl.semaphore_signal(barrier, inc=1, device_id={"sens": above}, device_id_type=MESH)

    @pl.when(not_first)
    def _():
        pl.semaphore_signal(barrier, inc=1, device_id={"sens": below}, device_id_type=MESH)

    pl.semaphore_wait(barrier, 1 + jnp.where(not_last, 1, 0) + jnp.where(not_first, 1, 0))

    build_window(lag_count, vectors, sig_ref, high, low)

    @pl.loop(0, half_rows // tile)
    def _(part):
        place = pl.ds(pl.multiple_of((1 - y) * half_rows + part * tile, tile), tile)
        adjoint_tile(k_ref[:, place], steps_count, high, low, p_ref, place)

        @pl.loop(0, tile // rows)
        def _(c):
            y_copy(part * (tile // rows) + c).start()

    @pl.loop(0, half_rows // tile)
    def _(part):
        place = pl.ds(pl.multiple_of(y * half_rows + part * tile, tile), tile)
        adjoint_tile(k_ref[:, place], steps_count, high, low, p_ref, place)

    lag_up, lag_down = HOP * z, HOP * (chain - 1 - z)
    lag_last = HOP * (chain - 1)

    @pl.loop(0, chunks + lag_last)
    def _(step):
        @pl.when(step < chunks)
        def _():
            y_copy(step).wait_recv()
            own[chunk(step)] = p_ref[half_chunk(y, step)] + y_in[chunk(step)]

        up = step - lag_up

        @pl.when((up >= 0) & (up < chunks))
        def _():
            @pl.when(not_first)
            def _():
                up_copy(up).wait_recv()

            @pl.when(jnp.logical_not(not_first))
            def _():
                up_in[chunk(up)] = jnp.zeros((rows, p_ref.shape[1]), jnp.float32)

            @pl.when(not_last)
            def _():
                up_out[chunk(up)] = own[chunk(up)] + up_in[chunk(up)]
                up_copy(up).start()

        down = step - lag_down

        @pl.when((down >= 0) & (down < chunks))
        def _():
            @pl.when(not_last)
            def _():
                down_copy(down).wait_recv()

            @pl.when(jnp.logical_not(not_last))
            def _():
                down_in[chunk(down)] = jnp.zeros((rows, p_ref.shape[1]), jnp.float32)

            @pl.when(not_first)
            def _():
                down_out[chunk(down)] = own[chunk(down)] + down_in[chunk(down)]
                down_copy(down).start()

        last = step - lag_last

        @pl.when((last >= 0) & (last < chunks))
        def _():
            total = own[chunk(last)] + up_in[chunk(last)] + down_in[chunk(last)]
            out_ref[half_chunk(y, last)] = smooth_rows(
                total, tap_ref[half_chunk(y, last)], steps_count
            )
            back_copy(last).start()

    def half_product(h):
        place = pl.ds(pl.multiple_of(h * half_rows, half_rows), half_rows)
        s_high[...], s_low[...] = split(out_ref[place, :])
        return place

    def group_product(group_rows, place, columns):
        k_high, k_low = split(k_ref[group_rows, place])
        dot = functools.partial(jnp.dot, preferred_element_type=jnp.float32)
        return dot(k_high, s_high[:, columns]) + (
            dot(k_high, s_low[:, columns]) + dot(k_low, s_high[:, columns])
        )

    group = min(8, k_ref.shape[0] // lag_count)
    group_size = group * lag_count
    group_count = k_ref.shape[0] // group_size
    spans = [slice(v * steps_count, (v + 1) * steps_count) for v in range(vectors)]
    mine = half_product(y)

    @pl.loop(0, group_count)
    def _(g):
        group_rows = pl.ds(pl.multiple_of(g * group_size, group_size), group_size)
        for columns in spans:
            product[group_rows, columns] = group_product(group_rows, mine, columns)

    @pl.loop(0, chunks)
    def _(c):
        back_wait(c)

    other = half_product(1 - y)
    time = lax.broadcasted_iota(jnp.int32, (lag_count, steps_count), 1)
    lag = lax.broadcasted_iota(jnp.int32, (lag_count, steps_count), 0)

    @pl.loop(0, group_count)
    def _(g):
        group_rows = pl.ds(pl.multiple_of(g * group_size, group_size), group_size)
        for vector, columns in enumerate(spans):
            total = product[group_rows, columns] + group_product(group_rows, other, columns)
            for sensor in range(group):
                part = total[sensor * lag_count : (sensor + 1) * lag_count]
                sheared = pltpu.roll(part, 0, 1, stride=1, stride_axis=0)
                row = jnp.sum(jnp.where(time >= lag, sheared, 0.0), axis=0, keepdims=True)
                data_ref[pl.ds((g * group + sensor) * vectors + vector, 1), :] = row

    @pl.loop(0, chunks)
    def _(c):
        y_copy(c).wait_send()
        back_copy(c).wait_send()

        @pl.when(not_last)
        def _():
            up_copy(c).wait_send()

        @pl.when(not_first)
        def _():
            down_copy(c).wait_send()


def summed_smoothed(series, kernel, taps, lag_count, vectors, sens_count):
    rows, unk_dev = kernel.shape
    columns = vectors * series.shape[1]
    tile = 128
    chunks = max(1, unk_dev // 2 // 32)
    half = pltpu.VMEM((unk_dev // 2, columns), jnp.float32)
    return pl.pallas_call(
        functools.partial(sum_kernel, sens_count // 2, chunks, lag_count, vectors, tile),
        out_shape=jax.ShapeDtypeStruct(series.shape, jnp.float32),
        in_specs=[pl.BlockSpec(memory_space=pltpu.VMEM)] * 3,
        out_specs=pl.BlockSpec(memory_space=pltpu.VMEM),
        scratch_shapes=[half] * 6
        + [pltpu.VMEM((unk_dev, columns), jnp.float32)] * 2
        + [pltpu.VMEM((rows, columns), jnp.bfloat16)] * 2
        + [pltpu.VMEM((unk_dev // 2, columns), jnp.bfloat16)] * 2
        + [pltpu.VMEM((rows, columns), jnp.float32)]
        + [pltpu.SemaphoreType.DMA((8, chunks))],
        compiler_params=pltpu.CompilerParams(
            collective_id=0, has_side_effects=True, vmem_limit_bytes=VMEM_LIMIT
        ),
    )(series, kernel, taps)


def gather_kernel(n, x_ref, out_ref, landed, send_sem, recv_sem):
    me = lax.axis_index("unk")
    width = x_ref.shape[1]
    greet("unk", [lax.rem(me + k, n) for k in range(1, n)])

    def copy(k):
        peer = lax.rem(me + k, n)
        return pltpu.make_async_remote_copy(
            src_ref=x_ref, dst_ref=landed.at[me],
            send_sem=send_sem.at[k], recv_sem=recv_sem.at[k],
            device_id={"unk": peer}, device_id_type=MESH)

    for k in range(1, n):
        copy(k).start()
    landed[me] = x_ref[...]
    for k in range(1, n):
        copy(k).wait_recv()
    for piece in range(n):
        out_ref[:, piece * width : (piece + 1) * width] = landed[piece]
    for k in range(1, n):
        copy(k).wait_send()


def gathered(part, n):
    rows, width = part.shape
    return pl.pallas_call(
        functools.partial(gather_kernel, n),
        out_shape=jax.ShapeDtypeStruct((rows, n * width), jnp.float32),
        in_specs=[pl.BlockSpec(memory_space=pltpu.VMEM)],
        out_specs=pl.BlockSpec(memory_space=pltpu.VMEM),
        scratch_shapes=[
            pltpu.VMEM((n, rows, width), jnp.float32),
            pltpu.SemaphoreType.DMA((n,)),
            pltpu.SemaphoreType.DMA((n,)),
        ],
        compiler_params=pltpu.CompilerParams(
            collective_id=2, has_side_effects=True, vmem_limit_bytes=VMEM_LIMIT
        ),
    )(part)


def scatter_kernel(n, x_ref, out_ref, stage, landed, send_sem, recv_sem):
    me = lax.axis_index("unk")
    width = out_ref.shape[1]
    greet("unk", [lax.rem(me + k, n) for k in range(1, n)])
    for piece in range(n):
        stage[piece] = x_ref[:, piece * width : (piece + 1) * width]

    def copy(k):
        peer = lax.rem(me + k, n)
        return pltpu.make_async_remote_copy(
            src_ref=stage.at[peer], dst_ref=landed.at[k],
            send_sem=send_sem.at[k], recv_sem=recv_sem.at[k],
            device_id={"unk": peer}, device_id_type=MESH)

    for k in range(1, n):
        copy(k).start()
    total = stage[me]
    for k in range(1, n):
        copy(k).wait_recv()
        total = total + landed[k]
    out_ref[...] = total
    for k in range(1, n):
        copy(k).wait_send()


def scattered(partial, n):
    rows, steps_count = partial.shape
    width = steps_count // n
    return pl.pallas_call(
        functools.partial(scatter_kernel, n),
        out_shape=jax.ShapeDtypeStruct((rows, width), jnp.float32),
        in_specs=[pl.BlockSpec(memory_space=pltpu.VMEM)],
        out_specs=pl.BlockSpec(memory_space=pltpu.VMEM),
        scratch_shapes=[
            pltpu.VMEM((n, rows, width), jnp.float32),
            pltpu.VMEM((n, rows, width), jnp.float32),
            pltpu.SemaphoreType.DMA((n,)),
            pltpu.SemaphoreType.DMA((n,)),
        ],
        compiler_params=pltpu.CompilerParams(
            collective_id=1, has_side_effects=True, vmem_limit_bytes=VMEM_LIMIT
        ),
    )(partial)


def on_device(signals, kernel, tap_weights, *, sens_count, unk_count):
    sens_rows, lag_count, unk_dev = kernel.shape
    _, vectors, width = signals.shape
    series = gathered(signals.reshape(sens_rows * vectors, width), unk_count)
    flat_kernel = kernel.reshape(sens_rows * lag_count, unk_dev)
    product = summed_smoothed(
        series, flat_kernel, tap_weights.T, lag_count, vectors, sens_count
    )
    return scattered(product, unk_count).reshape(signals.shape)


def solution(mesh):
    return jax.shard_map(
        functools.partial(
            on_device, sens_count=mesh.shape["sens"], unk_count=mesh.shape["unk"]
        ),
        mesh=mesh,
        in_specs=(P("sens", None, "unk"), P("sens", None, "unk"), P(None, "unk")),
        out_specs=P("sens", None, "unk"),
        check_vma=False,
    )
```
